32 devices in a mesh: dp: 4 (over y, x), expert: 8 (over z, core).
Axes of the slice: x: 2, y: 2, z: 4, core: 2. Of those that a mesh axis runs over, the one named last changes fastest.
Arguments:
- hidden_in: bfloat16 [32, 2, 2880], P(('expert', 'dp')), may hold values from -6 to 6
- queries: bfloat16 [32, 2, 4096], P(('expert', 'dp')), may hold values from -2 to 2
- new_keys: bfloat16 [32, 2, 512], P(('expert', 'dp')), may hold values from -2 to 2
- new_values: bfloat16 [32, 2, 512], P(('expert', 'dp')), may hold values from -6 to 6
- key_cache: bfloat16 [32, 512, 512], P(('expert', 'dp')), may hold values from -2 to 2
- value_cache: bfloat16 [32, 512, 512], P(('expert', 'dp')), may hold values from -6 to 6
- prompt_lengths: int32 [32], P(('expert', 'dp')), may hold values from 64 to 512, as said below
- out_weight: bfloat16 [4096, 2880], P('expert'), may hold values from -0.375 to 0.375
- norm_gain: float32 [2880], replicated, may hold values from 0.1 to 1.9
- expert_ids: int32 [32, 2, 4], P('expert'), may hold values from 0 to 15, all different within a row; in each aligned block of 8 rows (0 to 7, 8 to 15, ..., all dimensions but the last counted through in order) at most 6 rows name the same one
- top_logits: bfloat16 [32, 2, 4], P('expert'), may hold values from -4 to 4
- gate_weight: bfloat16 [16, 2880, 2880], P('expert', None, 'dp'), may hold values from -0.109375 to 0.109375
- up_weight: bfloat16 [16, 2880, 2880], P('expert', None, 'dp'), may hold values from -0.109375 to 0.109375
- down_weight: bfloat16 [16, 2880, 2880], P('expert', 'dp'), may hold values from -0.109375 to 0.109375
Outputs:
- layer_out: bfloat16 [32, 2, 2880], P(('expert', 'dp'))
The draws below stay inside these ranges and needn't reach their ends.
Inputs may be any that keep to these rules, and one draw needn't show every extreme that they name: `prompt_lengths`: some row has exactly 512 live slots. `expert_ids`: A row names 4 different experts at each position. Over the 4 rows held by one index of the expert axis and both positions, no expert is named more than 6 times, and in some such group one expert is named exactly 6 times.
All inputs are finite; a program needn't handle non-finite values.
Results may differ from the reference program's by a relative error of at most 0.02.
Values may be sent and summed in bfloat16 or wider, within the bound.
A program may use at most 128 MiB of HBM per device.

```python
import math
import jax
import jax.numpy as jnp
import numpy as np
from jax import lax

D = 2880
HQ = 64
KVH = 8
HD = 64
FF = 2880
TOPK = 4
STEPS = 2
LMAX = 512
EXPERTS = 16
COL_ROWS = 4
ROWS = 32
CAP = 6
N_DP = 4


def draw_prompt_lengths(key, part):
    first_key, second_key = jax.random.split(jax.random.fold_in(key, 7))
    lengths = jax.random.randint(first_key, (ROWS,), LMAX // 8, LMAX + 1)
    longest = jax.random.randint(second_key, (), 0, ROWS)
    return jnp.where(jnp.arange(ROWS) == longest, LMAX, lengths).astype(jnp.int32)


def block_levels(own_key, dims, cuts, smallest, top_value):
    factor_of, own = 1.0, jax.random.fold_in(own_key, 6)
    for dim, parts in cuts:
        steps = jnp.exp(jax.random.uniform(jax.random.fold_in(own, dim), (parts,), jnp.float32, smallest / len(cuts), top_value / len(cuts)))
        factor_of = factor_of * jnp.repeat(steps, dims[dim] // parts).reshape([-1 if axis == dim else 1 for axis in range(len(dims))])
    return factor_of


def assign_block(own_key, own, number, rows, count, top, reach, skew):
    ranking = jax.random.permutation(own_key, count)
    heavy_load, common = load_shares(count, rows * top, reach, skew, True), load_shares(count, rows * top, reach, skew, False)
    places = jnp.arange(count)

    def named(sizes, rotation):
        used = int((sizes > 0).sum())
        fixed = max(1, used // 4)
        moved = fixed + (places - fixed + rotation * (used - fixed)) % max(1, count - fixed)
        return jnp.zeros((count,), jnp.int32).at[ranking[jnp.where(places < fixed, places, moved)]].set(jnp.asarray(sizes, jnp.int32))

    sizes = jnp.where(number % 4 == 0, named(heavy_load, number // 4), named(common, number - number // 4 - 1))
    mixed = jax.random.permutation(jax.random.fold_in(own, 3), count)
    source_of, taker = mixed[0:count // 2 * 2:2], mixed[1:count // 2 * 2:2]
    slack = jnp.minimum(sizes[source_of] - 1, reach - sizes[taker]) // 2
    slack = jnp.where((source_of == ranking[0]) | (taker == ranking[0]) | (sizes[taker] == 0), 0, jnp.maximum(slack, 0))
    moved = jax.random.randint(jax.random.fold_in(own, 4), (count // 2,), 0, 1 << 20) % (slack + 1)
    sizes = sizes.at[source_of].add(-moved).at[taker].add(moved)
    members = jnp.searchsorted(jnp.cumsum(sizes), jnp.arange(rows * top), side="right").astype(jnp.int32)
    table = members.reshape(top, rows).T
    table = table[jax.random.permutation(jax.random.fold_in(own, 1), rows)]
    rotation = jax.random.randint(jax.random.fold_in(own, 2), (rows, 1), 0, top)
    return jnp.take_along_axis(table, (jnp.arange(top)[None, :] + rotation) % top, axis=1)


def load_shares(amount, total, reach, skew, full):
    weights = [(1 << 20) // math.isqrt(grade ** skew) + 1 for grade in range(1, amount + 1)]
    largest = reach if full else min(reach, max(-(-total // amount), total * weights[0] // sum(weights)))
    least = 1 if total - largest >= amount - 1 else 0
    given, surplus = [largest] + [least] * (amount - 1), total - largest - least * (amount - 1)
    while surplus > 0:
        movable = [i for i in range(1, amount) if given[i] < largest] or [i for i in range(1, amount) if given[i] < reach]
        pool, remaining = sum([weights[i] for i in movable]), surplus
        for i in movable:
            more = min(reach - given[i], max(1, remaining * weights[i] // pool), surplus)
            given[i] = given[i] + more
            surplus = surplus - more
    return np.array(given)


def centred(rng, extent, scale, most, cuts=(), kind=jnp.bfloat16):
    result = scale * jax.random.normal(rng, extent, jnp.float32)
    if cuts:
        result = result * block_levels(rng, extent, cuts, -0.22, 0.18)
    return jnp.clip(result, -most, most).astype(kind)


def setup_inputs(seed: int = 0) -> dict:
    arg_keys = jax.random.split(jax.random.key(seed), 15)
    hidden_in = centred(arg_keys[0], (ROWS, STEPS, D), 1.0, 6.0, ((0, 32),))
    queries = jnp.clip(jax.random.uniform(arg_keys[1], (ROWS, STEPS, HQ * HD), jnp.float32, -2.0, 2.0) * block_levels(arg_keys[1], (ROWS, STEPS, HQ * HD), ((0, 32),), -0.4, 0.0), -2.0, 2.0).astype(jnp.bfloat16)
    new_keys = jnp.clip(jax.random.uniform(arg_keys[2], (ROWS, STEPS, KVH * HD), jnp.float32, -2.0, 2.0) * block_levels(arg_keys[2], (ROWS, STEPS, KVH * HD), ((0, 32),), -0.4, 0.0), -2.0, 2.0).astype(jnp.bfloat16)
    new_values = centred(arg_keys[3], (ROWS, STEPS, KVH * HD), 1.0, 6.0, ((0, 32),))
    key_cache = jnp.clip(jax.random.uniform(arg_keys[4], (ROWS, LMAX, KVH * HD), jnp.float32, -2.0, 2.0) * block_levels(arg_keys[4], (ROWS, LMAX, KVH * HD), ((0, 32),), -0.4, 0.0), -2.0, 2.0).astype(jnp.bfloat16)
    value_cache = centred(arg_keys[5], (ROWS, LMAX, KVH * HD), 1.0, 6.0, ((0, 32),))
    prompt_lengths = draw_prompt_lengths(jax.random.fold_in(arg_keys[14], 71), 0)
    out_weight = centred(arg_keys[7], (HQ * HD, D), (HQ * HD // 16) ** -0.5, 0.375, ((0, 8),))
    norm_gain = jnp.clip(1.0 + 0.18 * jax.random.normal(arg_keys[8], (D,), jnp.float32), 0.1, 1.9)
    expert_ids_keys = jax.random.split(jax.random.fold_in(arg_keys[9], 1), ROWS * STEPS // (COL_ROWS * STEPS))
    expert_ids_turns = jax.random.permutation(jax.random.fold_in(arg_keys[9], 3), ROWS * STEPS // (COL_ROWS * STEPS))
    expert_ids = jax.vmap(lambda own, number: assign_block(jax.random.fold_in(arg_keys[9], 2), own, number, COL_ROWS * STEPS, EXPERTS, TOPK, CAP, 2))(expert_ids_keys, expert_ids_turns).reshape((ROWS, STEPS, TOPK))
    top_logits = centred(arg_keys[10], (ROWS, STEPS, TOPK), 1.0, 4.0, ((0, 8),))
    gate_weight = centred(arg_keys[11], (EXPERTS, D, FF), D ** -0.5, 0.109375, ((0, 8), (2, 4)))
    up_weight = centred(arg_keys[12], (EXPERTS, D, FF), D ** -0.5, 0.109375, ((0, 8), (2, 4)))
    down_weight = centred(arg_keys[13], (EXPERTS, FF, D), FF ** -0.5, 0.109375, ((0, 8), (1, 4)))
    return {"hidden_in": hidden_in, "queries": queries, "new_keys": new_keys, "new_values": new_values, "key_cache": key_cache, "value_cache": value_cache, "prompt_lengths": prompt_lengths, "out_weight": out_weight, "norm_gain": norm_gain, "expert_ids": expert_ids, "top_logits": top_logits, "gate_weight": gate_weight, "up_weight": up_weight, "down_weight": down_weight}


def attend_single(query_rows, fresh_keys, fresh_values, cache_keys, cache_values, length):
    step_count = query_rows.shape[0]
    cache_len = cache_keys.shape[0]
    keys_all = jnp.concatenate([cache_keys, fresh_keys], axis=0).astype(jnp.float32).reshape(cache_len + step_count, KVH, HD)
    values_all = jnp.concatenate([cache_values, fresh_values], axis=0).astype(jnp.float32).reshape(cache_len + step_count, KVH, HD)
    query_heads = query_rows.astype(jnp.float32).reshape(step_count, KVH, HQ // KVH, HD)
    scores = jnp.einsum('sgqe,kge->sgqk', query_heads, keys_all) * 0.125
    position = jnp.arange(cache_len + step_count, dtype=jnp.int32)
    step_ids = jnp.arange(step_count, dtype=jnp.int32)
    visible = (position[None, :] < length) | (position[None, :] >= cache_len) & (position[None, :] - cache_len <= step_ids[:, None])
    exp_scores = jnp.where(visible[:, None, None, :], jnp.exp(scores), jnp.zeros_like(scores))
    attn_probs = (exp_scores / lax.optimization_barrier(jnp.sum(exp_scores, axis=-1, keepdims=True))).astype(jnp.bfloat16)
    attended = jnp.einsum('sgqk,kge->sgqe', attn_probs.astype(jnp.float32), values_all)
    return attended.astype(jnp.bfloat16).reshape(step_count, HQ * HD)

def rms_normed(residual, norm_gain):
    inverse_rms = lax.rsqrt(lax.optimization_barrier(jnp.mean(residual * residual, axis=-1, keepdims=True)) + 1e-05)
    return (residual * inverse_rms * norm_gain).astype(jnp.bfloat16)

def swiglu_act(gate_vals, up_vals):
    return (gate_vals * jax.nn.sigmoid(1.702 * gate_vals) * (up_vals + 1.0)).astype(jnp.bfloat16)

def reference(hidden_in, queries, new_keys, new_values, key_cache, value_cache, prompt_lengths, out_weight, norm_gain, expert_ids, top_logits, gate_weight, up_weight, down_weight):
    attended = lax.map(lambda items: attend_single(*items), (queries, new_keys, new_values, key_cache, value_cache, prompt_lengths))
    flat_attn = attended.reshape(ROWS * STEPS, HQ * HD)
    projected = jnp.dot(flat_attn, out_weight, preferred_element_type=jnp.float32)
    residual = hidden_in.reshape(ROWS * STEPS, D).astype(jnp.float32) + projected
    normed = rms_normed(residual, norm_gain)
    flat_ids = expert_ids.reshape(ROWS * STEPS, TOPK)
    exp_logits = jnp.exp(top_logits.reshape(ROWS * STEPS, TOPK).astype(jnp.float32))
    mix_weights = exp_logits / lax.optimization_barrier(jnp.sum(exp_logits, axis=-1, keepdims=True))

    def expert_pass(running, inputs):
        gate_mat, up_mat, down_mat, expert_label = inputs
        gate_vals = jnp.dot(normed, gate_mat, preferred_element_type=jnp.float32)
        up_vals = jnp.dot(normed, up_mat, preferred_element_type=jnp.float32)
        activated = swiglu_act(gate_vals, up_vals)
        sliced = activated.astype(jnp.float32).reshape(ROWS * STEPS, N_DP, FF // N_DP)
        down_sliced = down_mat.astype(jnp.float32).reshape(N_DP, FF // N_DP, D)
        pieces = jnp.einsum('tjf,jfd->tjd', sliced, down_sliced).astype(jnp.bfloat16)
        expert_out = lax.optimization_barrier(jnp.sum(pieces.astype(jnp.float32), axis=1))
        token_share = lax.optimization_barrier(jnp.sum(jnp.where(flat_ids == expert_label, mix_weights, jnp.zeros_like(mix_weights)), axis=1))
        return (running + token_share[:, None] * expert_out, None)
    expert_labels = jnp.arange(EXPERTS, dtype=jnp.int32)
    moe_total = lax.scan(expert_pass, jnp.zeros((ROWS * STEPS, D), jnp.float32), (gate_weight, up_weight, down_weight, expert_labels))[0]
    return (residual + moe_total).astype(jnp.bfloat16).reshape(ROWS, STEPS, D)
```

```python
import functools

import jax
import jax.numpy as jnp
from jax import lax
from jax.experimental import pallas as pl
from jax.experimental.pallas import tpu as pltpu
from jax.sharding import PartitionSpec as P

KVH = 8
HD = 64
MESH = pl.DeviceIdType.MESH
F32 = jnp.float32
BF16 = jnp.bfloat16


def iota(shape, dim):
    return lax.broadcasted_iota(jnp.int32, shape, dim)


def dot_last(a, b):
    return lax.dot_general(a, b, (((1,), (1,)), ((), ())), preferred_element_type=F32)


def dot(a, b):
    return jnp.dot(a, b, preferred_element_type=F32)


def layer_kernel(
    n_dp, n_ex, per_index, cuts,
    plen_ref, hid_ref, q_ref, nk_ref, nv_ref, gain_ref, ids_ref, lg_ref,
    kc_hbm, vc_hbm, wo_hbm, wg_hbm, wu_hbm, wd_hbm,
    out_ref,
    kbuf, vbuf, wo, wg, wu, wd,
    qr, att, send_att, recv_att, xa, part, send_proj, recv_proj, resid,
    xbuf, xs, send_dp, recv_dp, send_out, recv_out,
    load_sem, ssem, rsem, fssem, frsem, hssem, hrsem,
):
    me_dp = lax.axis_index("dp")
    me_ex = lax.axis_index("expert")
    steps, width = hid_ref.shape[1], hid_ref.shape[2]
    feats = wo.shape[1]
    pad_at = xbuf.shape[3] - 128

    loads = [(kc_hbm.at[0], kbuf), (vc_hbm.at[0], vbuf), (wo_hbm, wo)]
    for l in range(per_index):
        loads += [(wg_hbm.at[l], wg.at[l]), (wu_hbm.at[l], wu.at[l]), (wd_hbm.at[l], wd.at[l])]
    loads = [pltpu.make_async_copy(s, d, load_sem.at[i]) for i, (s, d) in enumerate(loads)]
    for c in loads[:3]:
        c.start()

    barrier = pltpu.get_barrier_semaphore()
    for d in range(1, n_ex):
        pl.semaphore_signal(barrier, inc=1, device_id=(me_dp, lax.rem(me_ex + d, n_ex)), device_id_type=MESH)
    for d in range(1, n_dp):
        pl.semaphore_signal(barrier, inc=1, device_id=(lax.rem(me_dp + d, n_dp), me_ex), device_id_type=MESH)

    rows, lanes = 2 * KVH * 8, KVH * HD
    for g in range(KVH):
        qr[2 * g:2 * g + 2, :] = q_ref[0, :, g * lanes:(g + 1) * lanes].astype(F32)
    r_of, l_of = iota((rows, lanes), 0), iota((rows, lanes), 1)
    own_head = (l_of // HD) == (r_of % 8)
    own_group = (l_of // HD) == ((r_of % 64) // 8)
    repeat = ((iota((lanes, lanes), 0) % HD) == (iota((lanes, lanes), 1) % HD)).astype(F32).astype(BF16)
    er, ei = iota((rows, 16), 0), iota((rows, 16), 1)
    spread = (((er % 64) // 8 == ei // 2) & (er // 64 == ei % 2)).astype(F32).astype(BF16)
    fi, fr = iota((16, rows), 0), iota((16, rows), 1)
    collect = (((fr % 64) // 8 == fi // 2) & (fr // 64 == fi % 2)).astype(F32).astype(BF16)
    a = dot(spread, qr[...].astype(BF16))
    a = jnp.where(own_head, a, 0.0).astype(BF16)
    a = jnp.where(own_group, dot(a, repeat), 0.0).astype(BF16)
    nrow = iota((128, lanes), 0)

    def padded(ref):
        v = ref[0].astype(F32)
        return jnp.where(nrow == 0, v[0:1], jnp.where(nrow == 1, v[1:2], 0.0)).astype(BF16)

    sn = dot_last(a, padded(nk_ref)) * 0.125
    en = jnp.where(iota(sn.shape, 1) <= iota(sn.shape, 0) // 64, jnp.exp(sn), 0.0)
    loads[0].wait()
    sc = dot_last(a, kbuf[...]) * 0.125
    ec = jnp.where(iota(sc.shape, 1) < plen_ref[0], jnp.exp(sc), 0.0)
    den = jnp.sum(ec, axis=1, keepdims=True) + jnp.sum(en, axis=1, keepdims=True)
    loads[1].wait()
    for c in loads[3:]:
        c.start()
    o = dot((ec / den).astype(BF16), vbuf[...]) + dot((en / den).astype(BF16), padded(nv_ref))
    o = jnp.where(own_group, o, 0.0).astype(BF16)
    o = jnp.where(own_head, dot(o, repeat), 0.0).astype(BF16)
    att[...] = dot(collect, o)
    for e in range(n_ex):
        g, at = e * feats // lanes, e * feats % lanes
        send_att[e] = att[2 * g:2 * g + 2, at:at + feats].astype(BF16)
    recv_att[me_ex] = send_att[me_ex]

    pl.semaphore_wait(barrier, n_ex - 1 + n_dp - 1)

    def exchange(phase, send, recv):
        for d in range(1, n_ex):
            to = lax.rem(me_ex + d, n_ex)
            pltpu.make_async_remote_copy(
                send.at[to], recv.at[me_ex], ssem.at[phase, d], rsem.at[phase, me_ex],
                device_id=(me_dp, to), device_id_type=MESH,
            ).start()

    def exchanged(phase, send, recv):
        for d in range(1, n_ex):
            src = lax.rem(me_ex + d, n_ex)
            c = pltpu.make_async_remote_copy(
                send.at[src], recv.at[src], ssem.at[phase, d], rsem.at[phase, src],
                device_id=(me_dp, src), device_id_type=MESH,
            )
            c.wait_recv()
            c.wait_send()

    exchange(0, send_att, recv_att)

    logit = jnp.exp(lg_ref[me_dp].astype(F32))
    mix = logit / jnp.sum(logit, axis=1, keepdims=True)
    ids = ids_ref[me_dp]
    lane = iota((steps, 128), 1)
    dense = jnp.zeros((steps, 128), F32)
    for k in range(ids.shape[1]):
        dense = dense + jnp.where((lane % 64) == ids[:, k:k + 1], mix[:, k:k + 1], 0.0)
    high = dense.astype(BF16).astype(F32)
    dense = jnp.where(lane < 64, high, dense - high).astype(BF16)

    loads[2].wait()
    exchanged(0, send_att, recv_att)
    for e in range(n_ex):
        xa[2 * e:2 * e + 2, :] = recv_att[e].astype(F32)
    part[...] = dot_last(xa[...].astype(BF16), wo[...])
    for e in range(n_ex):
        send_proj[e] = part[2 * e:2 * e + 2, :].astype(BF16)
    recv_proj[me_ex] = send_proj[me_ex]
    exchange(1, send_proj, recv_proj)
    xbuf[me_dp, me_ex, :, width:pad_at] = jnp.zeros((steps, pad_at - width), BF16)
    xbuf[me_dp, me_ex, :, pad_at:] = dense
    exchanged(1, send_proj, recv_proj)
    res = hid_ref[0].astype(F32) + jnp.sum(recv_proj[...].astype(F32), axis=0)
    resid[...] = res
    inv = lax.rsqrt(jnp.sum(res * res, axis=1, keepdims=True) / width + 1e-05)
    xbuf[me_dp, me_ex, :, 0:width] = (res * inv * gain_ref[...].reshape(1, width)).astype(BF16)

    def to_expert(slab, d, peer):
        return pltpu.make_async_remote_copy(
            xbuf.at[me_dp, slab], xbuf.at[me_dp, slab], ssem.at[2, d], rsem.at[2, slab],
            device_id=(me_dp, peer), device_id_type=MESH,
        )

    def to_dp(row, slab, d, peer):
        return pltpu.make_async_remote_copy(
            xbuf.at[row, slab], xbuf.at[row, slab], fssem.at[slab, d], frsem.at[slab, row],
            device_id=(peer, me_ex), device_id_type=MESH,
        )

    def pass_on(slab):
        for d in range(1, n_dp):
            to_dp(me_dp, slab, d, lax.rem(me_dp + d, n_dp)).start()

    for d in range(1, n_ex):
        to_expert(me_ex, d, lax.rem(me_ex + d, n_ex)).start()
    pass_on(me_ex)
    for d in range(1, n_ex):
        src = lax.rem(me_ex + d, n_ex)
        to_expert(src, d, src).wait_recv()
        pass_on(src)
    for e in range(n_ex):
        xs[me_dp, 2 * e:2 * e + 2, :] = xbuf[me_dp, e].astype(F32)
    for d in range(1, n_dp):
        row = lax.rem(me_dp + d, n_dp)
        for e in range(n_ex):
            to_dp(row, e, d, row).wait_recv()
            xs[row, 2 * e:2 * e + 2, :] = xbuf[row, e].astype(F32)
    for d in range(1, n_ex):
        to_expert(me_ex, d, me_ex).wait_send()
    for d in range(1, n_dp):
        for e in range(n_ex):
            to_dp(me_dp, e, d, me_dp).wait_send()

    for c in loads[3:]:
        c.wait()
    span = max(1, min(n_dp, 64 // (2 * n_ex)))
    tokens = span * 2 * n_ex

    def block(at):
        x = xs[pl.ds(at, span), :, 0:width].reshape(tokens, width).astype(BF16)
        shares = xs[pl.ds(at, span), :, pad_at:].reshape(tokens, 128)
        lane_of = iota((tokens, 128), 1) % 64
        acts, parts = [], []
        for l in range(per_index):
            gate = dot_last(x, wg[l])
            up = dot_last(x, wu[l])
            acts.append((gate * jax.nn.sigmoid(1.702 * gate) * (up + 1.0)).astype(BF16))
            mine = lane_of == me_ex * per_index + l
            parts.append(jnp.sum(jnp.where(mine, shares, 0.0), axis=1, keepdims=True))
        for c, (lo, hi) in enumerate(cuts):
            total = dot(acts[0], wd[0, :, lo:hi]) * parts[0]
            for l in range(1, per_index):
                total = total + dot(acts[l], wd[l, :, lo:hi]) * parts[l]
            send_dp[c][pl.ds(at, span)] = total.reshape(span, 2 * n_ex, hi - lo).astype(BF16)
            if n_dp == span:
                scatter(c)

    def across(c, d, slot):
        to = lax.rem(me_dp + d, n_dp)
        return pltpu.make_async_remote_copy(
            send_dp[c].at[to], recv_dp[c].at[slot], hssem.at[c, d], hrsem.at[c, slot],
            device_id=(to, me_ex), device_id_type=MESH,
        )

    def scatter(c):
        for d in range(1, n_dp):
            across(c, d, me_dp).start()
        recv_dp[c][me_dp] = send_dp[c][me_dp]

    if n_dp == span:
        block(0)
    else:
        pl.loop(0, n_dp // span)(lambda i: block(i * span))
        for c in range(len(cuts)):
            scatter(c)

    for c, (lo, hi) in enumerate(cuts):
        for d in range(1, n_dp):
            across(c, d, lax.rem(me_dp + d, n_dp)).wait_recv()
        part[:, lo:hi] = jnp.sum(recv_dp[c][...].astype(F32), axis=0)
        for e in range(n_ex):
            send_out[c][e] = part[2 * e:2 * e + 2, lo:hi].astype(BF16)
        exchange(3 + c, send_out[c], recv_out[c])
        recv_out[c][me_ex] = send_out[c][me_ex]
    for c in range(len(cuts)):
        for d in range(1, n_dp):
            across(c, d, me_dp).wait_send()
    for c, (lo, hi) in enumerate(cuts):
        exchanged(3 + c, send_out[c], recv_out[c])
        moe = jnp.sum(recv_out[c][...].astype(F32), axis=0)
        out_ref[0, :, lo:hi] = (resid[:, lo:hi] + moe).astype(BF16)


def on_device(
    hidden_in, queries, new_keys, new_values, key_cache, value_cache, prompt_lengths,
    out_weight, norm_gain, expert_ids, top_logits, gate_weight, up_weight, down_weight,
):
    n_dp, n_ex = lax.axis_size("dp"), lax.axis_size("expert")
    per_index = gate_weight.shape[0]
    width = hidden_in.shape[2]
    feats = out_weight.shape[0]
    half = -(-width // 256) * 128
    cuts = ((0, half), (half, width))
    gate_weight, up_weight = jnp.swapaxes(gate_weight, 1, 2), jnp.swapaxes(up_weight, 1, 2)
    out_weight = out_weight.T
    padded = -(-width // 128) * 128 + 128
    toks = 2 * n_ex
    vm, anym = pl.BlockSpec(memory_space=pltpu.VMEM), pl.BlockSpec(memory_space=pl.ANY)
    dma = pltpu.SemaphoreType.DMA
    return pl.pallas_call(
        functools.partial(layer_kernel, n_dp, n_ex, per_index, cuts),
        out_shape=jax.ShapeDtypeStruct(hidden_in.shape, BF16),
        in_specs=[pl.BlockSpec(memory_space=pltpu.SMEM)] + [vm] * 7 + [anym] * 6,
        out_specs=vm,
        scratch_shapes=[
            pltpu.VMEM(key_cache.shape[1:], BF16),
            pltpu.VMEM(value_cache.shape[1:], BF16),
            pltpu.VMEM(out_weight.shape, BF16),
            pltpu.VMEM(gate_weight.shape, BF16),
            pltpu.VMEM(up_weight.shape, BF16),
            pltpu.VMEM(down_weight.shape, BF16),
            pltpu.VMEM((16, KVH * HD), F32),
            pltpu.VMEM((16, KVH * HD), F32),
            pltpu.VMEM((n_ex, 2, feats), BF16),
            pltpu.VMEM((n_ex, 2, feats), BF16),
            pltpu.VMEM((toks, feats), F32),
            pltpu.VMEM((toks, width), F32),
            pltpu.VMEM((n_ex, 2, width), BF16),
            pltpu.VMEM((n_ex, 2, width), BF16),
            pltpu.VMEM((2, width), F32),
            pltpu.VMEM((n_dp, n_ex, 2, padded), BF16),
            pltpu.VMEM((n_dp, toks, padded), F32),
            [pltpu.VMEM((n_dp, toks, hi - lo), BF16) for lo, hi in cuts],
            [pltpu.VMEM((n_dp, toks, hi - lo), BF16) for lo, hi in cuts],
            [pltpu.VMEM((n_ex, 2, hi - lo), BF16) for lo, hi in cuts],
            [pltpu.VMEM((n_ex, 2, hi - lo), BF16) for lo, hi in cuts],
            dma((3 + 3 * per_index,)),
            dma((5, n_ex)),
            dma((5, n_ex)),
            dma((n_ex, n_dp)),
            dma((n_ex, n_dp)),
            dma((2, n_dp)),
            dma((2, n_dp)),
        ],
        compiler_params=pltpu.CompilerParams(
            collective_id=0, has_side_effects=True, vmem_limit_bytes=58 * 1024 * 1024
        ),
        cost_estimate=pl.CostEstimate(flops=2 * 10**9, bytes_accessed=29 * 10**6, transcendentals=10**5),
    )(
        prompt_lengths, hidden_in, queries, new_keys, new_values, norm_gain,
        expert_ids, top_logits, key_cache, value_cache, out_weight,
        gate_weight, up_weight, down_weight,
    )


def solution(mesh):
    both = ("expert", "dp")
    placed = (
        P(both, None, None),
        P(both, None, None),
        P(both, None, None),
        P(both, None, None),
        P(both, None, None),
        P(both, None, None),
        P(both),
        P("expert", None),
        P(),
        P("expert", None, None),
        P("expert", None, None),
        P("expert", None, "dp"),
        P("expert", None, "dp"),
        P("expert", "dp", None),
    )
    return jax.shard_map(
        on_device,
        mesh=mesh,
        in_specs=placed,
        out_specs=P(both, None, None),
        check_vma=False,
    )
```

```python
import functools

import jax
import jax.numpy as jnp
from jax import lax
from jax.experimental import pallas as pl
from jax.experimental.pallas import tpu as pltpu
from jax.sharding import PartitionSpec as P

KVH = 8
HD = 64
MESH = pl.DeviceIdType.MESH
F32 = jnp.float32
BF16 = jnp.bfloat16


def iota(shape, dim):
    return lax.broadcasted_iota(jnp.int32, shape, dim)


def dot_last(a, b):
    return lax.dot_general(a, b, (((1,), (1,)), ((), ())), preferred_element_type=F32)


def dot(a, b):
    return jnp.dot(a, b, preferred_element_type=F32)


def layer_kernel(
    n_dp, n_ex, per_index, cuts,
    plen_ref, hid_ref, q_ref, nk_ref, nv_ref, gain_ref, ids_ref, lg_ref,
    kc_hbm, vc_hbm, wo_hbm, wg_hbm, wu_hbm, wd_hbm,
    out_ref,
    kbuf, vbuf, wo, wg, wu, wd,
    qr, att, send_att, recv_att, xa, part, send_proj, recv_proj, resid,
    xbuf, xs, xb, tot, send_twin, recv_twin, send_dp, recv_dp, send_out, recv_out,
    load_sem, ssem, rsem, fssem, frsem, tssem, trsem, hssem, hrsem,
):
    me_dp = lax.axis_index("dp")
    me_ex = lax.axis_index("expert")
    my_z, core = me_ex // 2, lax.rem(me_ex, 2)
    other, n_z = 1 - core, n_ex // 2
    per_blk = 16 // (2 * n_z)
    n_blk = n_dp // per_blk
    steps, width = hid_ref.shape[1], hid_ref.shape[2]
    feats = wo.shape[1]
    pad_at = xbuf.shape[3] - 128

    loads = [(kc_hbm.at[0], kbuf), (vc_hbm.at[0], vbuf), (wo_hbm, wo)]
    for l in range(per_index):
        loads += [(wg_hbm.at[l], wg.at[l]), (wu_hbm.at[l], wu.at[l]), (wd_hbm.at[l], wd.at[l])]
    loads = [pltpu.make_async_copy(s, d, load_sem.at[i]) for i, (s, d) in enumerate(loads)]
    for c in loads[:3]:
        c.start()

    barrier = pltpu.get_barrier_semaphore()
    for d in range(1, n_ex):
        pl.semaphore_signal(barrier, inc=1, device_id=(me_dp, lax.rem(me_ex + d, n_ex)), device_id_type=MESH)
    for d in range(1, n_dp):
        pl.semaphore_signal(barrier, inc=1, device_id=(lax.rem(me_dp + d, n_dp), me_ex), device_id_type=MESH)

    rows, lanes = 2 * KVH * 8, KVH * HD
    for g in range(KVH):
        qr[2 * g:2 * g + 2, :] = q_ref[0, :, g * lanes:(g + 1) * lanes].astype(F32)
    r_of, l_of = iota((rows, lanes), 0), iota((rows, lanes), 1)
    own_head = (l_of // HD) == (r_of % 8)
    own_group = (l_of // HD) == ((r_of % 64) // 8)
    repeat = ((iota((lanes, lanes), 0) % HD) == (iota((lanes, lanes), 1) % HD)).astype(F32).astype(BF16)
    er, ei = iota((rows, 16), 0), iota((rows, 16), 1)
    spread = (((er % 64) // 8 == ei // 2) & (er // 64 == ei % 2)).astype(F32).astype(BF16)
    fi, fr = iota((16, rows), 0), iota((16, rows), 1)
    collect = (((fr % 64) // 8 == fi // 2) & (fr // 64 == fi % 2)).astype(F32).astype(BF16)
    a = dot(spread, qr[...].astype(BF16))
    a = jnp.where(own_head, a, 0.0).astype(BF16)
    a = jnp.where(own_group, dot(a, repeat), 0.0).astype(BF16)
    nrow = iota((128, lanes), 0)

    def padded(ref):
        v = ref[0].astype(F32)
        return jnp.where(nrow == 0, v[0:1], jnp.where(nrow == 1, v[1:2], 0.0)).astype(BF16)

    sn = dot_last(a, padded(nk_ref)) * 0.125
    en = jnp.where(iota(sn.shape, 1) <= iota(sn.shape, 0) // 64, jnp.exp(sn), 0.0)
    loads[0].wait()
    sc = dot_last(a, kbuf[...]) * 0.125
    ec = jnp.where(iota(sc.shape, 1) < plen_ref[0], jnp.exp(sc), 0.0)
    den = jnp.sum(ec, axis=1, keepdims=True) + jnp.sum(en, axis=1, keepdims=True)
    loads[1].wait()
    for c in loads[3:]:
        c.start()
    o = dot((ec / den).astype(BF16), vbuf[...]) + dot((en / den).astype(BF16), padded(nv_ref))
    o = jnp.where(own_group, o, 0.0).astype(BF16)
    o = jnp.where(own_head, dot(o, repeat), 0.0).astype(BF16)
    att[...] = dot(collect, o)
    for e in range(n_ex):
        g, at = e * feats // lanes, e * feats % lanes
        send_att[e] = att[2 * g:2 * g + 2, at:at + feats].astype(BF16)
    recv_att[me_ex] = send_att[me_ex]

    pl.semaphore_wait(barrier, n_ex - 1 + n_dp - 1)

    def exchange(phase, send, recv):
        for d in range(1, n_ex):
            to = lax.rem(me_ex + d, n_ex)
            pltpu.make_async_remote_copy(
                send.at[to], recv.at[me_ex], ssem.at[phase, d], rsem.at[phase, me_ex],
                device_id=(me_dp, to), device_id_type=MESH,
            ).start()

    def exchanged(phase, send, recv):
        for d in range(1, n_ex):
            src = lax.rem(me_ex + d, n_ex)
            c = pltpu.make_async_remote_copy(
                send.at[src], recv.at[src], ssem.at[phase, d], rsem.at[phase, src],
                device_id=(me_dp, src), device_id_type=MESH,
            )
            c.wait_recv()
            c.wait_send()

    exchange(0, send_att, recv_att)

    logit = jnp.exp(lg_ref[me_dp].astype(F32))
    mix = logit / jnp.sum(logit, axis=1, keepdims=True)
    ids = ids_ref[me_dp]
    lane = iota((steps, 128), 1)
    dense = jnp.zeros((steps, 128), F32)
    for k in range(ids.shape[1]):
        dense = dense + jnp.where((lane % 64) == ids[:, k:k + 1], mix[:, k:k + 1], 0.0)
    high = dense.astype(BF16).astype(F32)
    dense = jnp.where(lane < 64, high, dense - high).astype(BF16)

    loads[2].wait()
    exchanged(0, send_att, recv_att)
    for e in range(n_ex):
        xa[2 * e:2 * e + 2, :] = recv_att[e].astype(F32)
    part[...] = dot_last(xa[...].astype(BF16), wo[...])
    for e in range(n_ex):
        send_proj[e] = part[2 * e:2 * e + 2, :].astype(BF16)
    recv_proj[me_ex] = send_proj[me_ex]
    exchange(1, send_proj, recv_proj)
    xbuf[me_dp, my_z, :, width:pad_at] = jnp.zeros((steps, pad_at - width), BF16)
    xbuf[me_dp, my_z, :, pad_at:] = dense
    exchanged(1, send_proj, recv_proj)
    res = hid_ref[0].astype(F32) + jnp.sum(recv_proj[...].astype(F32), axis=0)
    resid[...] = res
    inv = lax.rsqrt(jnp.sum(res * res, axis=1, keepdims=True) / width + 1e-05)
    xbuf[me_dp, my_z, :, 0:width] = (res * inv * gain_ref[...].reshape(1, width)).astype(BF16)

    def to_z(slab, d, peer):
        return pltpu.make_async_remote_copy(
            xbuf.at[me_dp, slab], xbuf.at[me_dp, slab], ssem.at[2, d], rsem.at[2, slab],
            device_id=(me_dp, 2 * peer + core), device_id_type=MESH,
        )

    def to_dp(row, slab, d, peer):
        return pltpu.make_async_remote_copy(
            xbuf.at[row, slab], xbuf.at[row, slab], fssem.at[slab, d], frsem.at[slab, row],
            device_id=(peer, me_ex), device_id_type=MESH,
        )

    def to_twin(half, b):
        return pltpu.make_async_remote_copy(
            xb.at[half * n_blk + b], xb.at[half * n_blk + b], tssem.at[b], trsem.at[b],
            device_id=(me_dp, 2 * my_z + other), device_id_type=MESH,
        )

    def pass_on(slab):
        for d in range(1, n_dp):
            to_dp(me_dp, slab, d, lax.rem(me_dp + d, n_dp)).start()

    for d in range(1, n_z):
        to_z(my_z, d, lax.rem(my_z + d, n_z)).start()
    pass_on(my_z)
    for d in range(1, n_z):
        src = lax.rem(my_z + d, n_z)
        to_z(src, d, src).wait_recv()
        pass_on(src)
    for d in range(n_dp):
        row = lax.rem(me_dp + d, n_dp)
        for z in range(n_z):
            if d > 0:
                to_dp(row, z, d, row).wait_recv()
            xs[d, 2 * z:2 * z + 2, :] = xbuf[row, z].astype(F32)
        if (d + 1) % per_blk == 0:
            b = d // per_blk
            xb[core * n_blk + b] = xs[b * per_blk:(b + 1) * per_blk].reshape(16, pad_at + 128).astype(BF16)
            to_twin(core, b).start()
    for d in range(1, n_z):
        to_z(my_z, d, my_z).wait_send()
    for d in range(1, n_dp):
        for z in range(n_z):
            to_dp(me_dp, z, d, me_dp).wait_send()
    for c in loads[3:]:
        c.wait()
    for b in range(n_blk):
        to_twin(other, b).wait_recv()
        to_twin(core, b).wait_send()

    span = min(2 * n_blk, 4)
    tokens = 16 * span

    def block(at):
        x = xb[pl.ds(at, span), :, 0:width].reshape(tokens, width)
        shares = xb[pl.ds(at, span), :, pad_at:].reshape(tokens, 128).astype(F32)
        lane_of = iota((tokens, 128), 1) % 64
        acts, parts = [], []
        for l in range(per_index):
            gate = dot_last(x, wg[l])
            up = dot_last(x, wu[l])
            acts.append((gate * jax.nn.sigmoid(1.702 * gate) * (up + 1.0)).astype(BF16))
            mine = lane_of == me_ex * per_index + l
            parts.append(jnp.sum(jnp.where(mine, shares, 0.0), axis=1, keepdims=True))
        for c, (lo, hi) in enumerate(cuts):
            total = dot(acts[0], wd[0, :, lo:hi]) * parts[0]
            for l in range(1, per_index):
                total = total + dot(acts[l], wd[l, :, lo:hi]) * parts[l]
            tot[c][pl.ds(at, span)] = total.reshape(span, 16, hi - lo)
            if 2 * n_blk == span:
                swap(c)

    def twin_sum(c):
        return pltpu.make_async_remote_copy(
            send_twin[c], recv_twin[c], tssem.at[n_blk + c], trsem.at[n_blk + c],
            device_id=(me_dp, 2 * my_z + other), device_id_type=MESH,
        )

    def swap(c):
        send_twin[c][...] = tot[c][pl.ds(other * n_blk, n_blk)].astype(BF16)
        twin_sum(c).start()

    def across(c, d, slot):
        return pltpu.make_async_remote_copy(
            send_dp[c].at[d], recv_dp[c].at[slot], hssem.at[c, d], hrsem.at[c, slot],
            device_id=(lax.rem(me_dp + d, n_dp), me_ex), device_id_type=MESH,
        )

    def along_z(c, d, to, slot):
        return pltpu.make_async_remote_copy(
            send_out[c].at[to], recv_out[c].at[slot], ssem.at[3 + c, d], rsem.at[3 + c, slot],
            device_id=(me_dp, 2 * to + core), device_id_type=MESH,
        )

    if 2 * n_blk == span:
        block(0)
    else:
        pl.loop(0, 2 * n_blk // span)(lambda i: block(i * span))
        for c in range(len(cuts)):
            swap(c)
    for c, (lo, hi) in enumerate(cuts):
        twin_sum(c).wait_recv()
        both = tot[c][pl.ds(core * n_blk, n_blk)] + recv_twin[c][...].astype(F32)
        send_dp[c][...] = both.reshape(n_dp, 2 * n_z, hi - lo).astype(BF16)
        for d in range(1, n_dp):
            across(c, d, me_dp).start()
        recv_dp[c][me_dp] = send_dp[c][0]
    for c, (lo, hi) in enumerate(cuts):
        for d in range(1, n_dp):
            across(c, d, lax.rem(me_dp + d, n_dp)).wait_recv()
        part[0:2 * n_z, lo:hi] = jnp.sum(recv_dp[c][...].astype(F32), axis=0)
        for z in range(n_z):
            send_out[c][z] = part[2 * z:2 * z + 2, lo:hi].astype(BF16)
        for d in range(1, n_z):
            along_z(c, d, lax.rem(my_z + d, n_z), my_z).start()
        recv_out[c][my_z] = send_out[c][my_z]
    for c, (lo, hi) in enumerate(cuts):
        twin_sum(c).wait_send()
        for d in range(1, n_dp):
            across(c, d, me_dp).wait_send()
    for c, (lo, hi) in enumerate(cuts):
        for d in range(1, n_z):
            src = lax.rem(my_z + d, n_z)
            along_z(c, d, src, src).wait_recv()
            along_z(c, d, src, src).wait_send()
        moe = jnp.sum(recv_out[c][...].astype(F32), axis=0)
        out_ref[0, :, lo:hi] = (resid[:, lo:hi] + moe).astype(BF16)


def on_device(
    hidden_in, queries, new_keys, new_values, key_cache, value_cache, prompt_lengths,
    out_weight, norm_gain, expert_ids, top_logits, gate_weight, up_weight, down_weight,
):
    n_dp, n_ex = lax.axis_size("dp"), lax.axis_size("expert")
    per_index = gate_weight.shape[0]
    width = hidden_in.shape[2]
    feats = out_weight.shape[0]
    half = -(-width // 256) * 128
    cuts = ((0, half), (half, width))
    gate_weight, up_weight = jnp.swapaxes(gate_weight, 1, 2), jnp.swapaxes(up_weight, 1, 2)
    out_weight = out_weight.T
    padded = -(-width // 128) * 128 + 128
    toks = 2 * n_ex
    n_z = n_ex // 2
    n_blk = n_dp * n_ex // 16
    vm, anym = pl.BlockSpec(memory_space=pltpu.VMEM), pl.BlockSpec(memory_space=pl.ANY)
    dma = pltpu.SemaphoreType.DMA
    return pl.pallas_call(
        functools.partial(layer_kernel, n_dp, n_ex, per_index, cuts),
        out_shape=jax.ShapeDtypeStruct(hidden_in.shape, BF16),
        in_specs=[pl.BlockSpec(memory_space=pltpu.SMEM)] + [vm] * 7 + [anym] * 6,
        out_specs=vm,
        scratch_shapes=[
            pltpu.VMEM(key_cache.shape[1:], BF16),
            pltpu.VMEM(value_cache.shape[1:], BF16),
            pltpu.VMEM(out_weight.shape, BF16),
            pltpu.VMEM(gate_weight.shape, BF16),
            pltpu.VMEM(up_weight.shape, BF16),
            pltpu.VMEM(down_weight.shape, BF16),
            pltpu.VMEM((16, KVH * HD), F32),
            pltpu.VMEM((16, KVH * HD), F32),
            pltpu.VMEM((n_ex, 2, feats), BF16),
            pltpu.VMEM((n_ex, 2, feats), BF16),
            pltpu.VMEM((toks, feats), F32),
            pltpu.VMEM((toks, width), F32),
            pltpu.VMEM((n_ex, 2, width), BF16),
            pltpu.VMEM((n_ex, 2, width), BF16),
            pltpu.VMEM((2, width), F32),
            pltpu.VMEM((n_dp, n_z, 2, padded), BF16),
            pltpu.VMEM((n_dp, n_ex, padded), F32),
            pltpu.VMEM((2 * n_blk, 16, padded), BF16),
            [pltpu.VMEM((2 * n_blk, 16, hi - lo), F32) for lo, hi in cuts],
            [pltpu.VMEM((n_blk, 16, hi - lo), BF16) for lo, hi in cuts],
            [pltpu.VMEM((n_blk, 16, hi - lo), BF16) for lo, hi in cuts],
            [pltpu.VMEM((n_dp, n_ex, hi - lo), BF16) for lo, hi in cuts],
            [pltpu.VMEM((n_dp, n_ex, hi - lo), BF16) for lo, hi in cuts],
            [pltpu.VMEM((n_z, 2, hi - lo), BF16) for lo, hi in cuts],
            [pltpu.VMEM((n_z, 2, hi - lo), BF16) for lo, hi in cuts],
            dma((3 + 3 * per_index,)),
            dma((5, n_ex)),
            dma((5, n_ex)),
            dma((n_z, n_dp)),
            dma((n_z, n_dp)),
            dma((n_blk + 2,)),
            dma((n_blk + 2,)),
            dma((2, n_dp)),
            dma((2, n_dp)),
        ],
        compiler_params=pltpu.CompilerParams(
            collective_id=0, has_side_effects=True, vmem_limit_bytes=58 * 1024 * 1024
        ),
        cost_estimate=pl.CostEstimate(flops=2 * 10**9, bytes_accessed=29 * 10**6, transcendentals=10**5),
    )(
        prompt_lengths, hidden_in, queries, new_keys, new_values, norm_gain,
        expert_ids, top_logits, key_cache, value_cache, out_weight,
        gate_weight, up_weight, down_weight,
    )


def solution(mesh):
    both = ("expert", "dp")
    placed = (
        P(both, None, None),
        P(both, None, None),
        P(both, None, None),
        P(both, None, None),
        P(both, None, None),
        P(both, None, None),
        P(both),
        P("expert", None),
        P(),
        P("expert", None, None),
        P("expert", None, None),
        P("expert", None, "dp"),
        P("expert", None, "dp"),
        P("expert", "dp", None),
    )
    return jax.shard_map(
        on_device,
        mesh=mesh,
        in_specs=placed,
        out_specs=P(both, None, None),
        check_vma=False,
    )
```
